1024 devices in a mesh: dp: 32 (over z, x_lo), ctx: 4 (over x_hi, core), tensor: 8 (over y).
Axes of the slice: x: 8 (x_hi: 2, x_lo: 4; x = x_hi * 4 + x_lo), y: 8, z: 8, core: 2. Of those that a mesh axis runs over, the one named last changes fastest.
Arguments:
- tokens: bfloat16 [20480, 7168], P(('dp', 'ctx'), 'tensor'), may hold values from -6 to 6
- routes: int32 [20480, 2], P(('dp', 'ctx')), may hold values from 0 to 31, all different within a row; in each aligned block of 160 rows (0 to 159, 160 to 319, ...) at most 12 rows name the same one
- route_weights: float32 [20480, 2], P(('dp', 'ctx')), may hold values from 0.1 to 1
- w_gate: bfloat16 [32, 7168, 1536], P('dp', 'tensor'), may hold values from -0.0625 to 0.0625
- w_up: bfloat16 [32, 7168, 1536], P('dp', 'tensor'), may hold values from -0.0625 to 0.0625
- w_down: bfloat16 [32, 1536, 7168], P('dp', None, 'tensor'), may hold values from -0.15625 to 0.15625
Outputs:
- combined: bfloat16 [20480, 7168], P(('dp', 'ctx'), 'tensor')
The draws below stay inside these ranges and needn't reach their ends.
Inputs may be any that keep to these rules, and one draw needn't show every extreme that they name: `routes`: each row names 2 different experts; within the rows of one group of 160 tokens no expert is named by more than 12 rows, and in some groups one expert is named by exactly 12 rows.
All inputs are finite; a program needn't handle non-finite values.
Results may differ from the reference program's by a relative error of at most 0.029.
Values may be sent and summed in bfloat16 or wider, within the bound.
A program may use at most 32 MiB of HBM per device.

```python
import math
import jax
import jax.numpy as jnp
import numpy as np
from jax import lax

D = 7168
H = 1536
TOK_GRP = 160
TOPK = 2
EXPERTS = 32
CAP = 12
TOKENS = 20480
N_TENSOR = 8


def block_levels(key, extent, shards, low, top_value):
    def one(position, parts):
        heights = jax.random.uniform(jax.random.fold_in(jax.random.fold_in(key, 6), position), (parts,), jnp.float32, low / len(shards), top_value / len(shards))
        return jnp.repeat(jnp.exp(heights), extent[position] // parts).reshape((-1,) + (1,) * (len(extent) - position - 1))

    gain = one(*shards[0])
    for cut in shards[1:]:
        gain = gain * one(*cut)
    return gain


def routed_block(key, own, number, rows, amount, top, limit, slope):
    order = jax.random.permutation(key, amount)
    heavy_load, usual = load_shares(amount, rows * top, limit, slope, True), load_shares(amount, rows * top, limit, slope, False)
    places = jnp.arange(amount)

    def named(lengths, turn):
        used = int((lengths > 0).sum())
        fixed = max(1, used // 4)
        passed = fixed + (places - fixed + turn * (used - fixed)) % max(1, amount - fixed)
        return jnp.zeros((amount,), jnp.int32).at[order[jnp.where(places < fixed, places, passed)]].set(jnp.asarray(lengths, jnp.int32))

    lengths = jnp.where(number % 4 == 0, named(heavy_load, number // 4), named(usual, number - number // 4 - 1))
    mixed = jax.random.permutation(jax.random.fold_in(own, 3), amount)
    donor, receiver = mixed[0:amount // 2 * 2:2], mixed[1:amount // 2 * 2:2]
    margin = jnp.minimum(lengths[donor] - 1, limit - lengths[receiver]) // 2
    margin = jnp.where((donor == order[0]) | (receiver == order[0]) | (lengths[receiver] == 0), 0, jnp.maximum(margin, 0))
    passed = jax.random.randint(jax.random.fold_in(own, 4), (amount // 2,), 0, 1 << 20) % (margin + 1)
    lengths = lengths.at[donor].add(-passed).at[receiver].add(passed)
    items = jnp.searchsorted(jnp.cumsum(lengths), jnp.arange(rows * top), side="right").astype(jnp.int32)
    table = items.reshape(top, rows).T
    table = table[jax.random.permutation(jax.random.fold_in(own, 1), rows)]
    turn = jax.random.randint(jax.random.fold_in(own, 2), (rows, 1), 0, top)
    return jnp.take_along_axis(table, (jnp.arange(top)[None, :] + turn) % top, axis=1)


def load_shares(count, total, limit, skew, full):
    portions = [(1 << 20) // math.isqrt(rank ** skew) + 1 for rank in range(1, count + 1)]
    largest = limit if full else min(limit, max(-(-total // count), total * portions[0] // sum(portions)))
    least = 1 if total - largest >= count - 1 else 0
    holding, spare = [largest] + [least] * (count - 1), total - largest - least * (count - 1)
    while spare > 0:
        movable = [i for i in range(1, count) if holding[i] < largest] or [i for i in range(1, count) if holding[i] < limit]
        whole, remaining = sum([portions[i] for i in movable]), spare
        for i in movable:
            more = min(limit - holding[i], max(1, remaining * portions[i] // whole), spare)
            holding[i] = holding[i] + more
            spare = spare - more
    return np.array(holding)


def noise(key, dims, width, reach, pieces=(), held_as=jnp.bfloat16):
    drawn = width * jax.random.normal(key, dims, jnp.float32)
    if pieces:
        drawn = drawn * block_levels(key, dims, pieces, -0.22, 0.18)
    return jnp.clip(drawn, -reach, reach).astype(held_as)


def setup_inputs(seed: int = 0) -> dict:
    key_of = jax.random.split(jax.random.key(seed), 7)
    tokens = noise(key_of[0], (TOKENS, D), 1.0, 6.0, ((0, 128), (1, 8)))
    routes_keys = jax.random.split(jax.random.fold_in(key_of[1], 1), TOKENS // TOK_GRP)
    routes_turns = jax.random.permutation(jax.random.fold_in(key_of[1], 3), TOKENS // TOK_GRP)
    routes = jax.vmap(lambda own, number: routed_block(jax.random.fold_in(key_of[1], 2), own, number, TOK_GRP, EXPERTS, TOPK, CAP, 2))(routes_keys, routes_turns).reshape((TOKENS, TOPK))
    route_weights = jnp.clip(jnp.exp(math.log(1.0) - 2.3025851 * jax.random.uniform(key_of[2], (TOKENS, TOPK), jnp.float32) ** block_levels(key_of[2], (TOKENS, TOPK), ((0, 128),), -0.2, 0.2)), 0.1, 1.0)
    w_gate = noise(key_of[3], (EXPERTS, D, H), D ** -0.5, 0.0625, ((0, 32), (1, 8)))
    w_up = noise(key_of[4], (EXPERTS, D, H), D ** -0.5, 0.0625, ((0, 32), (1, 8)))
    w_down = noise(key_of[5], (EXPERTS, H, D), H ** -0.5, 0.15625, ((0, 32), (2, 8)))
    return {"tokens": tokens, "routes": routes, "route_weights": route_weights, "w_gate": w_gate, "w_up": w_up, "w_down": w_down}


def rounded(values):
    narrow = lax.optimization_barrier(values.astype(jnp.bfloat16))
    return narrow.astype(jnp.float32)


def reference(tokens, routes, route_weights, w_gate, w_up, w_down):
    group_count = TOKENS // TOK_GRP
    assigned = routes.reshape(group_count, TOK_GRP * TOPK)
    onehot = (assigned[:, :, None] == jnp.arange(EXPERTS, dtype=jnp.int32)[None, None, :]).astype(jnp.int32)
    before = jnp.cumsum(onehot, axis=1) - onehot
    slot_index = jnp.sum(before * onehot, axis=2).reshape(-1).astype(jnp.int32)
    owner_rows = (jnp.arange(TOKENS * TOPK, dtype=jnp.int32) // TOPK).astype(jnp.int32)
    group_ids = (owner_rows // TOK_GRP).astype(jnp.int32)
    expert_ids = routes.reshape(-1).astype(jnp.int32)
    buffers = jnp.zeros((EXPERTS, group_count, CAP, D), jnp.bfloat16)
    buffers = buffers.at[expert_ids, group_ids, slot_index].set(tokens[owner_rows])
    block_width = D // N_TENSOR

    def one_expert(operands):
        slab, gate_mat, up_mat, down_mat = operands
        row_block = slab.reshape(group_count * CAP, N_TENSOR, block_width).astype(jnp.float32)
        gate_parts = jnp.einsum("rtd,tdh->trh", row_block, gate_mat.reshape(N_TENSOR, block_width, H).astype(jnp.float32))
        up_parts = jnp.einsum("rtd,tdh->trh", row_block, up_mat.reshape(N_TENSOR, block_width, H).astype(jnp.float32))
        gate_sum = jnp.sum(rounded(gate_parts), axis=0)
        up_sum = jnp.sum(rounded(up_parts), axis=0)
        activated = (jax.nn.silu(gate_sum) * up_sum).astype(jnp.bfloat16)
        projected = jnp.dot(activated, down_mat, preferred_element_type=jnp.float32).astype(jnp.bfloat16)
        return projected.reshape(group_count, CAP, D)

    results = lax.map(one_expert, (buffers, w_gate, w_up, w_down))
    picked = results[expert_ids, group_ids, slot_index].reshape(TOKENS, TOPK, D)
    running = jnp.zeros((TOKENS, D), jnp.float32)
    for which in range(TOPK):
        running = running + picked[:, which, :].astype(jnp.float32) * route_weights[:, which][:, None]
    return running.astype(jnp.bfloat16)
```

```python
import functools

import jax
import jax.numpy as jnp
from jax import lax
from jax.experimental import pallas as pl
from jax.experimental.pallas import tpu as pltpu
from jax.sharding import PartitionSpec as P

MESH = pl.DeviceIdType.MESH
BF16, F32 = jnp.bfloat16, jnp.float32

NZ, NX, NXL, NY = 8, 8, 4, 8
EXPERTS, CAP, TOK, TOPK = 32, 12, 160, 2
FEAT, HID = 896, 1536
SLOT, WIDE = 16, 768
TAIL = FEAT - WIDE
COLS = HID // 4

DZ_CHUNKS = ((1, 7), (2, 6), (3, 5), (0, 4))
NCH = len(DZ_CHUNKS)
ORDER = tuple((dz, dx) for pair in DZ_CHUNKS for dx in range(4) for dz in pair)
PER = len(ORDER) // NCH
ROWS = PER * CAP
PROWS = PER * SLOT
HALF = ROWS // 2
LAG = 2


def dot(a, b):
    return jnp.dot(a, b, preferred_element_type=F32)


def hops(c, d):
    return 4 if (c + d) % 2 == 0 else 3


def kernel(
    tok, rt, wt, wg_hbm, wu_hbm, wd_hbm, out,
    wg, wu, wd, pk, got, part, rs, act, rpk, ret, w_head, w_tail, acc,
    w_sem, d_send, d_recv, r_send, r_recv, s_send, s_recv, g_send, g_recv,
):
    dp, ctx, y = lax.axis_index("dp"), lax.axis_index("ctx"), lax.axis_index("tensor")
    z, xl = lax.div(dp, NXL), lax.rem(dp, NXL)
    xh, core = lax.div(ctx, 2), lax.rem(ctx, 2)
    x = xh * NXL + xl
    flip = lax.rem(lax.div(x, 2) + core, 2)
    x_far = lax.rem(x + NX + 2 - 4 * flip, NX)
    x_up, x_down = lax.rem(x + 1, NX), lax.rem(x + NX - 1, NX)

    def device(zz, xx):
        return (
            zz * NXL + lax.rem(xx, NXL),
            lax.div(xx, NXL) * 2 + core,
            y,
        )

    def target(dz, dx):
        return device(lax.rem(z + dz, NZ), (x, x_up, x_far, x_down)[dx])

    def source(dz, dx):
        return device(lax.rem(z + NZ - dz, NZ), (x, x_down, x_far, x_up)[dx])

    y_next = (dp, ctx, lax.rem(y + 1, NY))
    y_prev = (dp, ctx, lax.rem(y + NY - 1, NY))
    y_to = (y_next, y_prev)

    barrier = pltpu.get_barrier_semaphore()
    for dz, dx in ORDER:
        if (dz, dx) != (0, 0):
            pl.semaphore_signal(barrier, inc=1, device_id=target(dz, dx), device_id_type=MESH)
    for peer in y_to:
        pl.semaphore_signal(barrier, inc=1, device_id=peer, device_id_type=MESH)

    loads = [
        pltpu.make_async_copy(src.at[0], dst, w_sem.at[i])
        for i, (src, dst) in enumerate(((wg_hbm, wg), (wu_hbm, wu), (wd_hbm, wd)))
    ]
    for load in loads:
        load.start()

    block = lax.broadcasted_iota(jnp.int32, (EXPERTS, TOK), 0)
    expert = jnp.zeros((EXPERTS, TOK), jnp.int32)
    for p, (dz, dx) in enumerate(ORDER):
        e = lax.rem(z + dz, NZ) * NXL + lax.rem(xl + dx, NXL)
        expert = jnp.where(block == p, e, expert)
    first, second = rt[0:1, :] == expert, rt[1:2, :] == expert
    named = (first | second).astype(F32)
    earlier = (
        lax.broadcasted_iota(jnp.int32, (TOK, TOK), 0)
        < lax.broadcasted_iota(jnp.int32, (TOK, TOK), 1)
    ).astype(F32).astype(BF16)
    before = dot(named.astype(BF16), earlier)
    slot = jnp.where(first | second, before, -1.0).astype(BF16)
    weight = jnp.where(first, wt[0:1, :], jnp.where(second, wt[1:2, :], 0.0))
    weight_hi = weight.astype(BF16)
    weight_lo = (weight - weight_hi.astype(F32)).astype(BF16)
    spread = (
        lax.broadcasted_iota(jnp.int32, (EXPERTS * SLOT, EXPERTS), 0) // SLOT
        == lax.broadcasted_iota(jnp.int32, (EXPERTS * SLOT, EXPERTS), 1)
    ).astype(F32).astype(BF16)
    slots = dot(spread, slot)
    row = (lax.broadcasted_iota(jnp.int32, (EXPERTS * SLOT, TOK), 0) % SLOT).astype(F32)
    head = (slots == row) & (row < CAP)
    tails = [(slots == row - (CAP - 4 * i)) & (row >= CAP) for i in range(3)]
    pick = head.astype(F32).astype(BF16)
    picked = dot(pick, tok[:, :WIDE])
    rest = [dot(m.astype(F32).astype(BF16), tok[:, WIDE:]) for m in tails]
    for i in range(WIDE // 128):
        piece = picked[:, i * 128 : (i + 1) * 128]
        if i < 3:
            piece = piece + rest[i]
        pk[:, :, i * 128 : (i + 1) * 128] = piece.astype(BF16).reshape(EXPERTS, SLOT, 128)

    pl.semaphore_wait(barrier, len(ORDER) - 1 + len(y_to))

    for p, (dz, dx) in enumerate(ORDER):
        c = p // PER
        if (dz, dx) == (0, 0):
            pltpu.make_async_copy(pk.at[p], got.at[p], d_recv.at[c]).start()
        else:
            pltpu.make_async_remote_copy(
                src_ref=pk.at[p], dst_ref=got.at[p], send_sem=d_send.at[c], recv_sem=d_recv.at[c],
                device_id=target(dz, dx), device_id_type=MESH,
            ).start()

    heavy_hi, heavy_lo = dot(spread, weight_hi), dot(spread, weight_lo)
    for j, heavy in enumerate((heavy_hi, heavy_lo)):
        w_head[j] = jnp.where(head, heavy, 0.0).astype(BF16)
        for i in range(3):
            w_tail[j, i] = jnp.where(tails[i], heavy, 0.0).astype(BF16)
    acc[...] = jnp.zeros_like(acc)

    def places(shape, packed_axis):
        packed = lax.broadcasted_iota(jnp.int32, shape, packed_axis)
        plain = lax.broadcasted_iota(jnp.int32, shape, 1 - packed_axis)
        start, q = (packed // SLOT) * CAP, packed % SLOT
        kinds = [(plain == start + q) & (q < CAP)]
        kinds += [(plain == start + q - CAP + 4 * i) & (q >= CAP) for i in range(3)]
        return [k.astype(F32).astype(BF16) for k in kinds]

    unpack = places((ROWS, PROWS), 1)
    repack = places((PROWS, ROWS), 0)

    def owned(c, j):
        return act.at[c, pl.ds(lax.rem(j, 2) * HALF, HALF), pl.ds(pl.multiple_of(lax.div(j, 2) * COLS, COLS), COLS)]

    def owner(k, d):
        return lax.rem(y + k if d == 0 else y + NY - k, NY)

    def sum_copy(c, d, k, src):
        return pltpu.make_async_remote_copy(
            src_ref=src, dst_ref=rs.at[c, d, k - 1], send_sem=s_send.at[c, d, k - 1], recv_sem=s_recv.at[c, d, k - 1],
            device_id=y_to[d], device_id_type=MESH,
        )

    def gather_copy(c, d, k):
        piece = owned(c, owner(k - 1, 1 - d))
        return pltpu.make_async_remote_copy(
            src_ref=piece, dst_ref=piece, send_sem=g_send.at[c, d, k - 1], recv_sem=g_recv.at[c, d, k - 1],
            device_id=y_to[d], device_id_type=MESH,
        )

    def sum_src(c, d, k):
        return part.at[c, owner(hops(c, d), d)] if k == 1 else rs.at[c, d, k - 2]

    def stage_parts(c):
        span = pl.ds(c * PER, PER)
        pltpu.make_async_copy(got.at[span], got.at[span], d_recv.at[c]).wait()
        packed = got[c * PER : (c + 1) * PER].reshape(PROWS, WIDE)
        rows_head = dot(unpack[0], packed).astype(BF16)
        rows_tail = sum(dot(unpack[1 + i], packed[:, i * 128 : (i + 1) * 128]) for i in range(3)).astype(BF16)
        rows = jnp.concatenate([rows_head, rows_tail], axis=1)
        if c == 0:
            loads[0].wait()
            loads[1].wait()

        def columns(it, carry):
            cq = lax.rem(lax.div(y, 2) + 2 + it, 4)
            col = pl.ds(pl.multiple_of(cq * COLS, COLS), COLS)
            for h, w in enumerate((wg, wu)):
                sums = dot(rows, w[:, col]).astype(BF16)
                for rh in range(2):
                    part[c, 2 * cq + rh, h] = sums[rh * HALF : (rh + 1) * HALF]
            return carry

        lax.fori_loop(0, 4, columns, 0)
        for d in range(2):
            sum_copy(c, d, 1, sum_src(c, d, 1)).start()

    def stage_sum(c, k):
        for d in range(2):
            n = hops(c, d)
            if k > n:
                continue
            sum_copy(c, d, k - 1, sum_src(c, d, k - 1)).wait_recv()
            mine = part[c, owner(n - k + 1, d)].astype(F32)
            rs[c, d, k - 2] = (rs[c, d, k - 2].astype(F32) + mine).astype(BF16)
            sum_copy(c, d, k, sum_src(c, d, k)).start()

    def stage_act(c):
        total = part[c, y].astype(F32)
        for d in range(2):
            n = hops(c, d)
            sum_copy(c, d, n, sum_src(c, d, n)).wait_recv()
            total = total + rs[c, d, n - 1].astype(F32)
        gate, up = total[0], total[1]
        owned(c, y)[...] = (gate / (1.0 + jnp.exp(-gate)) * up).astype(BF16)
        for d in range(2):
            gather_copy(c, d, 1).start()

    def stage_gather(c, k):
        for d in range(2):
            if k > hops(c, d):
                continue
            gather_arrival(c, d, k - 1).wait_recv()
            gather_copy(c, d, k).start()

    def gather_arrival(c, d, k):
        piece = owned(c, owner(k, 1 - d))
        return pltpu.make_async_remote_copy(
            src_ref=piece, dst_ref=piece, send_sem=g_send.at[c, d, k - 1], recv_sem=g_recv.at[c, d, k - 1],
            device_id=y_to[d], device_id_type=MESH,
        )

    def stage_down(c):
        for d in range(2):
            gather_arrival(c, d, hops(c, d)).wait_recv()
        if c == 0:
            loads[2].wait()
        given = dot(act[c], wd[...]).astype(BF16)
        heads = dot(repack[0], given[:, :WIDE])
        for i in range(WIDE // 128):
            piece = heads[:, i * 128 : (i + 1) * 128]
            if i < 3:
                piece = piece + dot(repack[1 + i], given[:, WIDE:])
            rpk[c * PER : (c + 1) * PER, :, i * 128 : (i + 1) * 128] = piece.astype(BF16).reshape(PER, SLOT, 128)
        for p in range(c * PER, (c + 1) * PER):
            dz, dx = ORDER[p]
            if (dz, dx) == (0, 0):
                pltpu.make_async_copy(rpk.at[p], ret.at[p], r_recv.at[c]).start()
            else:
                pltpu.make_async_remote_copy(
                    src_ref=rpk.at[p], dst_ref=ret.at[p], send_sem=r_send.at[c], recv_sem=r_recv.at[c],
                    device_id=source(dz, dx), device_id_type=MESH,
                ).start()

    def stage_combine(c):
        span = pl.ds(c * PER, PER)
        pltpu.make_async_copy(ret.at[span], ret.at[span], r_recv.at[c]).wait()
        packed = ret[c * PER : (c + 1) * PER].reshape(PROWS, WIDE)
        here = slice(c * PROWS, (c + 1) * PROWS)

        def turned(weights, values):
            return lax.dot_general(weights, values, (((0,), (0,)), ((), ())), preferred_element_type=F32)

        acc[:, :WIDE] += turned(w_head[0, here], packed) + turned(w_head[1, here], packed)
        acc[:, WIDE:] += sum(
            turned(w_tail[j, i, here], packed[:, i * 128 : (i + 1) * 128]) for j in range(2) for i in range(3)
        )

    stages = (
        stage_parts,
        functools.partial(stage_sum, k=2), functools.partial(stage_sum, k=3), functools.partial(stage_sum, k=4),
        stage_act,
        functools.partial(stage_gather, k=2), functools.partial(stage_gather, k=3), functools.partial(stage_gather, k=4),
        stage_down,
    )
    for tick in range(LAG * (NCH - 1) + len(stages)):
        for c in range(NCH):
            if 0 <= tick - LAG * c < len(stages):
                stages[tick - LAG * c](c)
    for c in range(NCH):
        stage_combine(c)
    out[...] = acc[...].astype(BF16)

    for c in range(NCH):
        remote = sum(ORDER[p] != (0, 0) for p in range(c * PER, (c + 1) * PER))
        span = pl.ds(c * PER, remote)
        pltpu.make_async_copy(pk.at[span], pk.at[span], d_send.at[c]).wait()
        pltpu.make_async_copy(rpk.at[span], rpk.at[span], r_send.at[c]).wait()
        for d in range(2):
            for k in range(1, hops(c, d) + 1):
                sum_copy(c, d, k, sum_src(c, d, k)).wait_send()
                gather_copy(c, d, k).wait_send()


def on_device(tokens, routes, route_weights, w_gate, w_up, w_down):
    vmem = pl.BlockSpec(memory_space=pltpu.VMEM)
    hbm = pl.BlockSpec(memory_space=pltpu.HBM)
    dma = pltpu.SemaphoreType.DMA
    return pl.pallas_call(
        kernel,
        out_shape=jax.ShapeDtypeStruct((TOK, FEAT), BF16),
        in_specs=[vmem, vmem, vmem, hbm, hbm, hbm],
        out_specs=vmem,
        scratch_shapes=[
            pltpu.VMEM((FEAT, HID), BF16),
            pltpu.VMEM((FEAT, HID), BF16),
            pltpu.VMEM((HID, FEAT), BF16),
            pltpu.VMEM((EXPERTS, SLOT, WIDE), BF16),
            pltpu.VMEM((EXPERTS, SLOT, WIDE), BF16),
            pltpu.VMEM((NCH, NY, 2, HALF, COLS), BF16),
            pltpu.VMEM((NCH, 2, 4, 2, HALF, COLS), BF16),
            pltpu.VMEM((NCH, ROWS, HID), BF16),
            pltpu.VMEM((EXPERTS, SLOT, WIDE), BF16),
            pltpu.VMEM((EXPERTS, SLOT, WIDE), BF16),
            pltpu.VMEM((2, EXPERTS * SLOT, TOK), BF16),
            pltpu.VMEM((2, 3, EXPERTS * SLOT, TOK), BF16),
            pltpu.VMEM((TOK, FEAT), F32),
            dma((3,)),
            dma((NCH,)), dma((NCH,)), dma((NCH,)), dma((NCH,)),
            dma((NCH, 2, 4)), dma((NCH, 2, 4)), dma((NCH, 2, 4)), dma((NCH, 2, 4)),
        ],
        compiler_params=pltpu.CompilerParams(
            collective_id=0, has_side_effects=True, vmem_limit_bytes=48 * 1024 * 1024
        ),
        cost_estimate=pl.CostEstimate(flops=3_200_000_000, bytes_accessed=9_000_000, transcendentals=600_000),
    )(tokens, routes.T, route_weights.T, w_gate, w_up, w_down)


def solution(mesh):
    in_specs = (
        P(("dp", "ctx"), "tensor"),
        P(("dp", "ctx"), None),
        P(("dp", "ctx"), None),
        P("dp", "tensor", None),
        P("dp", "tensor", None),
        P("dp", None, "tensor"),
    )
    return jax.shard_map(
        on_device, mesh=mesh, in_specs=in_specs, out_specs=P(("dp", "ctx"), "tensor"), check_vma=False
    )
```

```python
import functools

import jax
import jax.numpy as jnp
from jax import lax
from jax.experimental import pallas as pl
from jax.experimental.pallas import tpu as pltpu
from jax.sharding import PartitionSpec as P

MESH = pl.DeviceIdType.MESH
BF16, F32 = jnp.bfloat16, jnp.float32

NZ, NX, NXL, NY = 8, 8, 4, 8
EXPERTS, CAP, TOK, TOPK = 32, 12, 160, 2
FEAT, HID = 896, 1536
SLOT, WIDE = 16, 768
TAIL = FEAT - WIDE
COLS = HID // 4

CHUNKS = (
    ((0, 0), (0, 1), (0, 2), (0, 3), (1, 0), (7, 0), (1, 1), (7, 1)),
    ((3, 0), (5, 0), (3, 2), (5, 2), (4, 1), (4, 3), (2, 2), (6, 2)),
    ((3, 1), (5, 1), (3, 3), (5, 3), (4, 0), (4, 2), (2, 3), (6, 3)),
    ((1, 2), (7, 2), (1, 3), (7, 3), (2, 0), (6, 0), (2, 1), (6, 1)),
)
NCH = len(CHUNKS)
ORDER = tuple(offset for chunk in CHUNKS for offset in chunk)
PER = len(ORDER) // NCH
ROWS = PER * CAP
PROWS = PER * SLOT
HALF = ROWS // 2
LAG = 1


def dot(a, b):
    return jnp.dot(a, b, preferred_element_type=F32)


def hops(c, d):
    return 4 if (c + d) % 2 == 0 else 3


def kernel(
    tok_hbm, rt_hbm, wt_hbm, wg_hbm, wu_hbm, wd_hbm, out,
    tok, rt, wt, wg, wu, wd, pk, got, part, rs, act, rpk, ret, w_head, w_tail, acc,
    w_sem, d_send, d_recv, r_send, r_recv, s_send, s_recv, g_send, g_recv,
):
    dp, ctx, y = lax.axis_index("dp"), lax.axis_index("ctx"), lax.axis_index("tensor")
    z, xl = lax.div(dp, NXL), lax.rem(dp, NXL)
    xh, core = lax.div(ctx, 2), lax.rem(ctx, 2)
    x = xh * NXL + xl
    flip = lax.rem(lax.div(x, 2) + core, 2)
    x_far = lax.rem(x + NX + 2 - 4 * flip, NX)
    x_up, x_down = lax.rem(x + 1, NX), lax.rem(x + NX - 1, NX)

    def device(zz, xx):
        return (
            zz * NXL + lax.rem(xx, NXL),
            lax.div(xx, NXL) * 2 + core,
            y,
        )

    def target(dz, dx):
        return device(lax.rem(z + dz, NZ), (x, x_up, x_far, x_down)[dx])

    def source(dz, dx):
        return device(lax.rem(z + NZ - dz, NZ), (x, x_down, x_far, x_up)[dx])

    y_next = (dp, ctx, lax.rem(y + 1, NY))
    y_prev = (dp, ctx, lax.rem(y + NY - 1, NY))
    y_to = (y_next, y_prev)

    inputs = [
        pltpu.make_async_copy(src, dst, w_sem.at[3 + i])
        for i, (src, dst) in enumerate(((rt_hbm, rt), (wt_hbm, wt), (tok_hbm, tok)))
    ]
    loads = [
        pltpu.make_async_copy(src.at[0], dst, w_sem.at[i])
        for i, (src, dst) in enumerate(((wg_hbm, wg), (wu_hbm, wu), (wd_hbm, wd)))
    ]

    for load in inputs + loads:
        load.start()
    barrier = pltpu.get_barrier_semaphore()
    for dz, dx in ORDER:
        if (dz, dx) != (0, 0):
            pl.semaphore_signal(barrier, inc=1, device_id=target(dz, dx), device_id_type=MESH)
    for peer in y_to:
        pl.semaphore_signal(barrier, inc=1, device_id=peer, device_id_type=MESH)

    for load in inputs:
        load.wait()
    block = lax.broadcasted_iota(jnp.int32, (EXPERTS, TOK), 0)
    expert = jnp.zeros((EXPERTS, TOK), jnp.int32)
    for p, (dz, dx) in enumerate(ORDER):
        e = lax.rem(z + dz, NZ) * NXL + lax.rem(xl + dx, NXL)
        expert = jnp.where(block == p, e, expert)
    first, second = rt[0:1, :] == expert, rt[1:2, :] == expert
    named = (first | second).astype(F32)
    earlier = (
        lax.broadcasted_iota(jnp.int32, (TOK, TOK), 0)
        < lax.broadcasted_iota(jnp.int32, (TOK, TOK), 1)
    ).astype(F32).astype(BF16)
    before = dot(named.astype(BF16), earlier)
    slot = jnp.where(first | second, before, -1.0)
    weight = jnp.where(first, wt[0:1, :], jnp.where(second, wt[1:2, :], 0.0))
    q = lax.broadcasted_iota(jnp.int32, (PER, SLOT, TOK), 1).reshape(PROWS, TOK).astype(F32)
    filled = {}

    def repeat(values):
        return jnp.broadcast_to(values[:, None, :], (PER, SLOT, TOK)).reshape(PROWS, TOK)

    def one_hot(mask):
        return mask.astype(F32).astype(BF16)

    def stage_fill(c):
        mine = slice(c * PER, (c + 1) * PER)
        slots = repeat(slot[mine])
        head = slots == q
        tails = [(slots == q - (CAP - 4 * i)) & (q >= CAP) for i in range(3)]
        picked = dot(one_hot(head), tok[:, :WIDE])
        for i in range(WIDE // 128):
            piece = picked[:, i * 128 : (i + 1) * 128]
            if i < 3:
                piece = piece + dot(one_hot(tails[i]), tok[:, WIDE:])
            pk[mine, :, i * 128 : (i + 1) * 128] = piece.astype(BF16).reshape(PER, SLOT, 128)
        filled[c] = head, tails

    def stage_dispatch(c):
        for p in range(c * PER, (c + 1) * PER):
            dz, dx = ORDER[p]
            if (dz, dx) == (0, 0):
                pltpu.make_async_copy(pk.at[p], got.at[p], d_recv.at[c]).start()
            else:
                pltpu.make_async_remote_copy(
                    src_ref=pk.at[p], dst_ref=got.at[p], send_sem=d_send.at[c], recv_sem=d_recv.at[c],
                    device_id=target(dz, dx), device_id_type=MESH,
                ).start()
        head, tails = filled.pop(c)
        heavy = repeat(weight[c * PER : (c + 1) * PER])
        here = slice(c * PROWS, (c + 1) * PROWS)
        heavy_hi = heavy.astype(BF16).astype(F32)
        for j, part_of in enumerate((heavy_hi, heavy - heavy_hi)):
            w_head[j, here] = jnp.where(head, part_of, 0.0).astype(BF16)
            for i in range(3):
                w_tail[j, i, here] = jnp.where(tails[i], part_of, 0.0).astype(BF16)

    def sent(sem, ref, c):
        remote = sum(ORDER[p] != (0, 0) for p in range(c * PER, (c + 1) * PER))
        span = pl.ds(c * PER, remote)
        pltpu.make_async_copy(ref.at[span], ref.at[span], sem.at[c]).wait()

    stage_fill(0)
    pl.semaphore_wait(barrier, len(ORDER) - 1 + len(y_to))
    stage_dispatch(0)
    stage_fill(1)
    acc[...] = jnp.zeros_like(acc)

    def places(shape, packed_axis):
        packed = lax.broadcasted_iota(jnp.int32, shape, packed_axis)
        plain = lax.broadcasted_iota(jnp.int32, shape, 1 - packed_axis)
        start, q = (packed // SLOT) * CAP, packed % SLOT
        kinds = [(plain == start + q) & (q < CAP)]
        kinds += [(plain == start + q - CAP + 4 * i) & (q >= CAP) for i in range(3)]
        return [k.astype(F32).astype(BF16) for k in kinds]

    unpack = places((ROWS, PROWS), 1)
    repack = places((PROWS, ROWS), 0)

    def owned(c, j):
        return act.at[c, pl.ds(lax.rem(j, 2) * HALF, HALF), pl.ds(pl.multiple_of(lax.div(j, 2) * COLS, COLS), COLS)]

    def owner(k, d):
        return lax.rem(y + k if d == 0 else y + NY - k, NY)

    def sum_copy(c, d, k, src):
        return pltpu.make_async_remote_copy(
            src_ref=src, dst_ref=rs.at[c, d, k - 1], send_sem=s_send.at[c, d, k - 1], recv_sem=s_recv.at[c, d, k - 1],
            device_id=y_to[d], device_id_type=MESH,
        )

    def gather_copy(c, d, k):
        piece = owned(c, owner(k - 1, 1 - d))
        return pltpu.make_async_remote_copy(
            src_ref=piece, dst_ref=piece, send_sem=g_send.at[c, d, k - 1], recv_sem=g_recv.at[c, d, k - 1],
            device_id=y_to[d], device_id_type=MESH,
        )

    def sum_src(c, d, k):
        return part.at[c, owner(hops(c, d), d)] if k == 1 else rs.at[c, d, k - 2]

    def stage_parts(c):
        span = pl.ds(c * PER, PER)
        pltpu.make_async_copy(got.at[span], got.at[span], d_recv.at[c]).wait()
        packed = got[c * PER : (c + 1) * PER].reshape(PROWS, WIDE)
        rows_head = dot(unpack[0], packed).astype(BF16)
        rows_tail = sum(dot(unpack[1 + i], packed[:, i * 128 : (i + 1) * 128]) for i in range(3)).astype(BF16)
        rows = jnp.concatenate([rows_head, rows_tail], axis=1)
        if c == 0:
            loads[0].wait()
            loads[1].wait()

        def columns(it, carry):
            cq = lax.rem(lax.div(y, 2) + 2 - c % 2 + it, 4)
            col = pl.ds(pl.multiple_of(cq * COLS, COLS), COLS)
            for h, w in enumerate((wg, wu)):
                sums = dot(rows, w[:, col]).astype(BF16)
                for rh in range(2):
                    part[c, 2 * cq + rh, h] = sums[rh * HALF : (rh + 1) * HALF]
            return carry

        lax.fori_loop(0, 2, columns, 0)
        for d in range(2):
            sum_copy(c, d, 1, sum_src(c, d, 1)).start()
        lax.fori_loop(2, 4, columns, 0)

    def stage_sum(c, k):
        for d in range(2):
            n = hops(c, d)
            if k > n:
                continue
            sum_copy(c, d, k - 1, sum_src(c, d, k - 1)).wait_recv()
            mine = part[c, owner(n - k + 1, d)].astype(F32)
            rs[c, d, k - 2] = (rs[c, d, k - 2].astype(F32) + mine).astype(BF16)
            sum_copy(c, d, k, sum_src(c, d, k)).start()

    def stage_act(c):
        total = part[c, y].astype(F32)
        for d in range(2):
            n = hops(c, d)
            sum_copy(c, d, n, sum_src(c, d, n)).wait_recv()
            total = total + rs[c, d, n - 1].astype(F32)
        gate, up = total[0], total[1]
        owned(c, y)[...] = (gate / (1.0 + jnp.exp(-gate)) * up).astype(BF16)
        for d in range(2):
            gather_copy(c, d, 1).start()

    def stage_gather(c, k):
        for d in range(2):
            if k > hops(c, d):
                continue
            gather_arrival(c, d, k - 1).wait_recv()
            gather_copy(c, d, k).start()

    def gather_arrival(c, d, k):
        piece = owned(c, owner(k, 1 - d))
        return pltpu.make_async_remote_copy(
            src_ref=piece, dst_ref=piece, send_sem=g_send.at[c, d, k - 1], recv_sem=g_recv.at[c, d, k - 1],
            device_id=y_to[d], device_id_type=MESH,
        )

    def stage_down(c):
        for d in range(2):
            gather_arrival(c, d, hops(c, d)).wait_recv()
        if c == 0:
            loads[2].wait()
        given = dot(act[c], wd[...]).astype(BF16)
        heads = dot(repack[0], given[:, :WIDE])
        for i in range(WIDE // 128):
            piece = heads[:, i * 128 : (i + 1) * 128]
            if i < 3:
                piece = piece + dot(repack[1 + i], given[:, WIDE:])
            rpk[c * PER : (c + 1) * PER, :, i * 128 : (i + 1) * 128] = piece.astype(BF16).reshape(PER, SLOT, 128)
        for p in range(c * PER, (c + 1) * PER):
            dz, dx = ORDER[p]
            if (dz, dx) == (0, 0):
                pltpu.make_async_copy(rpk.at[p], ret.at[p], r_recv.at[c]).start()
            else:
                pltpu.make_async_remote_copy(
                    src_ref=rpk.at[p], dst_ref=ret.at[p], send_sem=r_send.at[c], recv_sem=r_recv.at[c],
                    device_id=source(dz, dx), device_id_type=MESH,
                ).start()

    def stage_combine(c):
        span = pl.ds(c * PER, PER)
        pltpu.make_async_copy(ret.at[span], ret.at[span], r_recv.at[c]).wait()
        packed = ret[c * PER : (c + 1) * PER].reshape(PROWS, WIDE)
        here = slice(c * PROWS, (c + 1) * PROWS)

        def turned(weights, values):
            return lax.dot_general(weights, values, (((0,), (0,)), ((), ())), preferred_element_type=F32)

        acc[:, :WIDE] += turned(w_head[0, here], packed) + turned(w_head[1, here], packed)
        acc[:, WIDE:] += sum(
            turned(w_tail[j, i, here], packed[:, i * 128 : (i + 1) * 128]) for j in range(2) for i in range(3)
        )

    stages = (
        stage_parts,
        functools.partial(stage_sum, k=2), functools.partial(stage_sum, k=3), functools.partial(stage_sum, k=4),
        stage_act,
        functools.partial(stage_gather, k=2), functools.partial(stage_gather, k=3), functools.partial(stage_gather, k=4),
        stage_down,
    )
    for tick in range(LAG * (NCH - 1) + len(stages)):
        if tick < NCH - 1:
            sent(d_send, pk, tick)
            stage_dispatch(tick + 1)
        for c in range(NCH):
            if 0 <= tick - LAG * c < len(stages):
                stages[tick - LAG * c](c)
        if tick < NCH - 2:
            stage_fill(tick + 2)
    for c in range(NCH):
        stage_combine(c)
    out[...] = acc[...].astype(BF16)

    for c in range(NCH):
        if c == NCH - 1:
            sent(d_send, pk, c)
        sent(r_send, rpk, c)
        for d in range(2):
            for k in range(1, hops(c, d) + 1):
                sum_copy(c, d, k, sum_src(c, d, k)).wait_send()
                gather_copy(c, d, k).wait_send()


def on_device(tokens, routes, route_weights, w_gate, w_up, w_down):
    vmem = pl.BlockSpec(memory_space=pltpu.VMEM)
    hbm = pl.BlockSpec(memory_space=pltpu.HBM)
    dma = pltpu.SemaphoreType.DMA
    return pl.pallas_call(
        kernel,
        out_shape=jax.ShapeDtypeStruct((TOK, FEAT), BF16),
        in_specs=[hbm] * 6,
        out_specs=vmem,
        scratch_shapes=[
            pltpu.VMEM((TOK, FEAT), BF16),
            pltpu.VMEM((TOPK, TOK), jnp.int32),
            pltpu.VMEM((TOPK, TOK), F32),
            pltpu.VMEM((FEAT, HID), BF16),
            pltpu.VMEM((FEAT, HID), BF16),
            pltpu.VMEM((HID, FEAT), BF16),
            pltpu.VMEM((EXPERTS, SLOT, WIDE), BF16),
            pltpu.VMEM((EXPERTS, SLOT, WIDE), BF16),
            pltpu.VMEM((NCH, NY, 2, HALF, COLS), BF16),
            pltpu.VMEM((NCH, 2, 4, 2, HALF, COLS), BF16),
            pltpu.VMEM((NCH, ROWS, HID), BF16),
            pltpu.VMEM((EXPERTS, SLOT, WIDE), BF16),
            pltpu.VMEM((EXPERTS, SLOT, WIDE), BF16),
            pltpu.VMEM((2, EXPERTS * SLOT, TOK), BF16),
            pltpu.VMEM((2, 3, EXPERTS * SLOT, TOK), BF16),
            pltpu.VMEM((TOK, FEAT), F32),
            dma((6,)),
            dma((NCH,)), dma((NCH,)), dma((NCH,)), dma((NCH,)),
            dma((NCH, 2, 4)), dma((NCH, 2, 4)), dma((NCH, 2, 4)), dma((NCH, 2, 4)),
        ],
        compiler_params=pltpu.CompilerParams(
            collective_id=0, has_side_effects=True, vmem_limit_bytes=60 * 1024 * 1024
        ),
        cost_estimate=pl.CostEstimate(flops=3_200_000_000, bytes_accessed=9_000_000, transcendentals=600_000),
    )(tokens, routes.T, route_weights.T, w_gate, w_up, w_down)


def solution(mesh):
    in_specs = (
        P(("dp", "ctx"), "tensor"),
        P(("dp", "ctx"), None),
        P(("dp", "ctx"), None),
        P("dp", "tensor", None),
        P("dp", "tensor", None),
        P("dp", None, "tensor"),
    )
    return jax.shard_map(
        on_device, mesh=mesh, in_specs=in_specs, out_specs=P(("dp", "ctx"), "tensor"), check_vma=False
    )
```

```python
import functools

import jax
import jax.numpy as jnp
from jax import lax
from jax.experimental import pallas as pl
from jax.experimental.pallas import tpu as pltpu
from jax.sharding import PartitionSpec as P

MESH = pl.DeviceIdType.MESH
BF16, F32 = jnp.bfloat16, jnp.float32

NZ, NX, NXL, NY = 8, 8, 4, 8
EXPERTS, CAP, TOK, TOPK = 32, 12, 160, 2
FEAT, HID = 896, 1536
SLOT, WIDE = 16, 768
TAIL = FEAT - WIDE
COLS = HID // 4

CHUNKS = (
    ((0, 0), (0, 1), (0, 2), (0, 3), (1, 0), (7, 0), (1, 1), (7, 1)),
    ((4, 1), (4, 3), (3, 2), (5, 2), (3, 0), (5, 0), (2, 2), (6, 2)),
    ((4, 2), (4, 0), (3, 3), (5, 3), (3, 1), (5, 1), (2, 3), (6, 3)),
    ((2, 0), (6, 0), (2, 1), (6, 1), (1, 2), (7, 2), (1, 3), (7, 3)),
)
NCH = len(CHUNKS)
ORDER = tuple(offset for chunk in CHUNKS for offset in chunk)
PER = len(ORDER) // NCH
ROWS = PER * CAP
PROWS = PER * SLOT
HALF = ROWS // 2
START = (0, 1, 3, 3)


def dot(a, b):
    return jnp.dot(a, b, preferred_element_type=F32)


def hops(c, d):
    return 4 if (c + d) % 2 == 0 else 3


def kernel(
    tok_hbm, rt_hbm, wt_hbm, wg_hbm, wu_hbm, wd_hbm, out,
    tok, rt, wt, wg, wu, wd, pk, got, part, rs, act, rpk, ret, w_head, w_tail, acc,
    w_sem, d_send, d_recv, r_send, r_recv, s_send, s_recv, g_send, g_recv,
):
    dp, ctx, y = lax.axis_index("dp"), lax.axis_index("ctx"), lax.axis_index("tensor")
    z, xl = lax.div(dp, NXL), lax.rem(dp, NXL)
    xh, core = lax.div(ctx, 2), lax.rem(ctx, 2)
    x = xh * NXL + xl
    turn = 1 - 2 * core
    flip = lax.rem(lax.div(x, 2) + core, 2)
    x_far = lax.rem(x + NX + 2 - 4 * flip, NX)
    x_up, x_down = lax.rem(x + 1, NX), lax.rem(x + NX - 1, NX)

    def device(zz, xx):
        return (
            zz * NXL + lax.rem(xx, NXL),
            lax.div(xx, NXL) * 2 + core,
            y,
        )

    def target(dz, dx):
        return device(lax.rem(z + dz, NZ), (x, x_up, x_far, x_down)[dx])

    def source(dz, dx):
        return device(lax.rem(z + NZ - dz, NZ), (x, x_down, x_far, x_up)[dx])

    y_others = [(dp, ctx, lax.rem(y + k, NY)) for k in (1, NY - 1)]

    barrier = pltpu.get_barrier_semaphore()
    for dz, dx in sorted(ORDER, key=lambda o: -min(o[0], NZ - o[0]) - min(o[1], NXL - o[1])):
        if (dz, dx) != (0, 0):
            pl.semaphore_signal(barrier, inc=1, device_id=target(dz, dx), device_id_type=MESH)
    for peer in y_others:
        pl.semaphore_signal(barrier, inc=1, device_id=peer, device_id_type=MESH)

    inputs = [
        pltpu.make_async_copy(src, dst, w_sem.at[3 + i])
        for i, (src, dst) in enumerate(((rt_hbm, rt), (wt_hbm, wt), (tok_hbm, tok)))
    ]
    loads = [
        pltpu.make_async_copy(src.at[0], dst, w_sem.at[i])
        for i, (src, dst) in enumerate(((wg_hbm, wg), (wu_hbm, wu), (wd_hbm, wd)))
    ]

    for load in inputs + loads:
        load.start()
    for load in inputs:
        load.wait()
    block = lax.broadcasted_iota(jnp.int32, (EXPERTS, TOK), 0)
    expert = jnp.zeros((EXPERTS, TOK), jnp.int32)
    for p, (dz, dx) in enumerate(ORDER):
        e = lax.rem(z + dz, NZ) * NXL + lax.rem(xl + dx, NXL)
        expert = jnp.where(block == p, e, expert)
    first, second = rt[0:1, :] == expert, rt[1:2, :] == expert
    named = (first | second).astype(F32)
    earlier = (
        lax.broadcasted_iota(jnp.int32, (TOK, TOK), 0)
        < lax.broadcasted_iota(jnp.int32, (TOK, TOK), 1)
    ).astype(F32).astype(BF16)
    before = dot(named.astype(BF16), earlier)
    slot = jnp.where(first | second, before, -1.0)
    weight = jnp.where(first, wt[0:1, :], jnp.where(second, wt[1:2, :], 0.0))
    q = lax.broadcasted_iota(jnp.int32, (PER, SLOT, TOK), 1).reshape(PROWS, TOK).astype(F32)

    def repeat(values):
        return jnp.broadcast_to(values[:, None, :], (PER, SLOT, TOK)).reshape(PROWS, TOK)

    def masks(c):
        slots = repeat(slot[c * PER : (c + 1) * PER])
        return slots == q, [(slots == q - (CAP - 4 * i)) & (q >= CAP) for i in range(3)]

    def one_hot(mask):
        return mask.astype(F32).astype(BF16)

    def stage_fill(c):
        mine = slice(c * PER, (c + 1) * PER)
        head, tails = masks(c)
        picked = dot(one_hot(head), tok[:, :WIDE])
        for i in range(WIDE // 128):
            piece = picked[:, i * 128 : (i + 1) * 128]
            if i < 3:
                piece = piece + dot(one_hot(tails[i]), tok[:, WIDE:])
            pk[mine, :, i * 128 : (i + 1) * 128] = piece.astype(BF16).reshape(PER, SLOT, 128)

    def stage_dispatch(c):
        for p in range(c * PER, (c + 1) * PER):
            dz, dx = ORDER[p]
            if (dz, dx) == (0, 0):
                pltpu.make_async_copy(pk.at[p], got.at[p], d_recv.at[c]).start()
            else:
                pltpu.make_async_remote_copy(
                    src_ref=pk.at[p], dst_ref=got.at[p], send_sem=d_send.at[c], recv_sem=d_recv.at[c],
                    device_id=target(dz, dx), device_id_type=MESH,
                ).start()

    def stage_weights(c):
        head, tails = masks(c)
        heavy = repeat(weight[c * PER : (c + 1) * PER])
        here = slice(c * PROWS, (c + 1) * PROWS)
        heavy_hi = heavy.astype(BF16).astype(F32)
        for j, part_of in enumerate((heavy_hi, heavy - heavy_hi)):
            w_head[j, here] = jnp.where(head, part_of, 0.0).astype(BF16)
            for i in range(3):
                w_tail[j, i, here] = jnp.where(tails[i], part_of, 0.0).astype(BF16)

    def sent(sem, ref, c):
        remote = sum(ORDER[p] != (0, 0) for p in range(c * PER, (c + 1) * PER))
        span = pl.ds(c * PER, remote)
        pltpu.make_async_copy(ref.at[span], ref.at[span], sem.at[c]).wait()

    stage_fill(0)
    stage_fill(1)
    pl.semaphore_wait(barrier, len(ORDER) - 1 + len(y_others))
    stage_dispatch(0)
    sent(d_send, pk, 0)
    stage_dispatch(1)
    for c in range(2, NCH):
        stage_fill(c)

    def places(shape, packed_axis):
        packed = lax.broadcasted_iota(jnp.int32, shape, packed_axis)
        plain = lax.broadcasted_iota(jnp.int32, shape, 1 - packed_axis)
        start, q = (packed // SLOT) * CAP, packed % SLOT
        kinds = [(plain == start + q) & (q < CAP)]
        kinds += [(plain == start + q - CAP + 4 * i) & (q >= CAP) for i in range(3)]
        return [k.astype(F32).astype(BF16) for k in kinds]

    unpack = places((ROWS, PROWS), 1)
    repack = places((PROWS, ROWS), 0)

    def owned(c, j):
        return act.at[c, j]

    def owner(k, d):
        return lax.rem(y + NY + turn * (k if d == 0 else -k), NY)

    y_to = [(dp, ctx, owner(1, d)) for d in range(2)]

    def sum_copy(c, d, k, src):
        return pltpu.make_async_remote_copy(
            src_ref=src, dst_ref=rs.at[c, d, k - 1], send_sem=s_send.at[c, d, k - 1], recv_sem=s_recv.at[c, d, k - 1],
            device_id=y_to[d], device_id_type=MESH,
        )

    def gather_copy(c, d, k):
        piece = owned(c, owner(k - 1, 1 - d))
        return pltpu.make_async_remote_copy(
            src_ref=piece, dst_ref=piece, send_sem=g_send.at[c, d, k - 1], recv_sem=g_recv.at[c, d, k - 1],
            device_id=y_to[d], device_id_type=MESH,
        )

    def sum_src(c, d, k):
        return part.at[c, owner(hops(c, d), d)] if k == 1 else rs.at[c, d, k - 2]

    def stage_parts(c):
        if c == 1:
            sent(d_send, pk, 1)
            for later in range(2, NCH):
                stage_dispatch(later)
        span = pl.ds(c * PER, PER)
        pltpu.make_async_copy(got.at[span], got.at[span], d_recv.at[c]).wait()
        packed = got[c * PER : (c + 1) * PER].reshape(PROWS, WIDE)
        rows_head = dot(unpack[0], packed).astype(BF16)
        rows_tail = sum(dot(unpack[1 + i], packed[:, i * 128 : (i + 1) * 128]) for i in range(3)).astype(BF16)
        rows = jnp.concatenate([rows_head, rows_tail], axis=1)
        if c == 0:
            loads[0].wait()
            loads[1].wait()

        def columns(it, carry):
            cq = lax.rem(lax.div(y, 2) + 1 + lax.rem(y, 2) + it, 4)
            col = pl.ds(pl.multiple_of(cq * COLS, COLS), COLS)
            for h, w in enumerate((wg, wu)):
                sums = dot(rows, w[:, col]).astype(BF16)
                for rh in range(2):
                    part[c, 2 * cq + rh, h] = sums[rh * HALF : (rh + 1) * HALF]
            return carry

        lax.fori_loop(0, 2, columns, 0)
        for d in range(2):
            sum_copy(c, d, 1, sum_src(c, d, 1)).start()
        lax.fori_loop(2, 4, columns, 0)

    def stage_sum(c, k):
        for d in range(2):
            n = hops(c, d)
            if k > n:
                continue
            sum_copy(c, d, k - 1, sum_src(c, d, k - 1)).wait_recv()
            mine = part[c, owner(n - k + 1, d)].astype(F32)
            rs[c, d, k - 2] = (rs[c, d, k - 2].astype(F32) + mine).astype(BF16)
            sum_copy(c, d, k, sum_src(c, d, k)).start()

    def stage_act(c):
        total = part[c, y].astype(F32)
        for d in range(2):
            n = hops(c, d)
            sum_copy(c, d, n, sum_src(c, d, n)).wait_recv()
            total = total + rs[c, d, n - 1].astype(F32)
        gate, up = total[0], total[1]
        owned(c, y)[...] = (gate / (1.0 + jnp.exp(-gate)) * up).astype(BF16)
        for d in range(2):
            gather_copy(c, d, 1).start()

    def stage_gather(c, k):
        for d in range(2):
            if k > hops(c, d):
                continue
            gather_arrival(c, d, k - 1).wait_recv()
            gather_copy(c, d, k).start()

    def gather_arrival(c, d, k):
        piece = owned(c, owner(k, 1 - d))
        return pltpu.make_async_remote_copy(
            src_ref=piece, dst_ref=piece, send_sem=g_send.at[c, d, k - 1], recv_sem=g_recv.at[c, d, k - 1],
            device_id=y_to[d], device_id_type=MESH,
        )

    def stage_down(c):
        for d in range(2):
            gather_arrival(c, d, hops(c, d)).wait_recv()
        if c == 0:
            loads[2].wait()
        hidden = jnp.concatenate([act[c, j : j + 2].reshape(ROWS, COLS) for j in range(0, NY, 2)], axis=1)
        given = dot(hidden, wd[...]).astype(BF16)
        heads = dot(repack[0], given[:, :WIDE])
        for i in range(WIDE // 128):
            piece = heads[:, i * 128 : (i + 1) * 128]
            if i < 3:
                piece = piece + dot(repack[1 + i], given[:, WIDE:])
            rpk[c * PER : (c + 1) * PER, :, i * 128 : (i + 1) * 128] = piece.astype(BF16).reshape(PER, SLOT, 128)
        for p in range(c * PER, (c + 1) * PER):
            dz, dx = ORDER[p]
            if (dz, dx) == (0, 0):
                pltpu.make_async_copy(rpk.at[p], ret.at[p], r_recv.at[c]).start()
            else:
                pltpu.make_async_remote_copy(
                    src_ref=rpk.at[p], dst_ref=ret.at[p], send_sem=r_send.at[c], recv_sem=r_recv.at[c],
                    device_id=source(dz, dx), device_id_type=MESH,
                ).start()

    def stage_combine(c):
        span = pl.ds(c * PER, PER)
        pltpu.make_async_copy(ret.at[span], ret.at[span], r_recv.at[c]).wait()
        packed = ret[c * PER : (c + 1) * PER].reshape(PROWS, WIDE)
        here = slice(c * PROWS, (c + 1) * PROWS)

        def turned(weights, values):
            return lax.dot_general(weights, values, (((0,), (0,)), ((), ())), preferred_element_type=F32)

        acc[:, :WIDE] += turned(w_head[0, here], packed) + turned(w_head[1, here], packed)
        acc[:, WIDE:] += sum(
            turned(w_tail[j, i, here], packed[:, i * 128 : (i + 1) * 128]) for j in range(2) for i in range(3)
        )

    stages = (
        stage_parts,
        functools.partial(stage_sum, k=2), functools.partial(stage_sum, k=3), functools.partial(stage_sum, k=4),
        stage_act,
        functools.partial(stage_gather, k=2), functools.partial(stage_gather, k=3), functools.partial(stage_gather, k=4),
        stage_down,
    )
    for tick in range(max(START) + len(stages)):
        for c in range(NCH):
            i = tick - START[c]
            if 0 <= i < len(stages):
                stages[i](c)
    for c in range(NCH):
        stage_weights(c)
    acc[...] = jnp.zeros_like(acc)
    for c in range(NCH):
        stage_combine(c)
    out[...] = acc[...].astype(BF16)

    for c in range(NCH):
        if c >= 2:
            sent(d_send, pk, c)
        sent(r_send, rpk, c)
        for d in range(2):
            for k in range(1, hops(c, d) + 1):
                sum_copy(c, d, k, sum_src(c, d, k)).wait_send()
                gather_copy(c, d, k).wait_send()


def on_device(tokens, routes, route_weights, w_gate, w_up, w_down):
    vmem = pl.BlockSpec(memory_space=pltpu.VMEM)
    hbm = pl.BlockSpec(memory_space=pltpu.HBM)
    dma = pltpu.SemaphoreType.DMA
    return pl.pallas_call(
        kernel,
        out_shape=jax.ShapeDtypeStruct((TOK, FEAT), BF16),
        in_specs=[hbm] * 6,
        out_specs=vmem,
        scratch_shapes=[
            pltpu.VMEM((TOK, FEAT), BF16),
            pltpu.VMEM((TOPK, TOK), jnp.int32),
            pltpu.VMEM((TOPK, TOK), F32),
            pltpu.VMEM((FEAT, HID), BF16),
            pltpu.VMEM((FEAT, HID), BF16),
            pltpu.VMEM((HID, FEAT), BF16),
            pltpu.VMEM((EXPERTS, SLOT, WIDE), BF16),
            pltpu.VMEM((EXPERTS, SLOT, WIDE), BF16),
            pltpu.VMEM((NCH, NY, 2, HALF, COLS), BF16),
            pltpu.VMEM((NCH, 2, 4, 2, HALF, COLS), BF16),
            pltpu.VMEM((NCH, NY, HALF, COLS), BF16),
            pltpu.VMEM((EXPERTS, SLOT, WIDE), BF16),
            pltpu.VMEM((EXPERTS, SLOT, WIDE), BF16),
            pltpu.VMEM((2, EXPERTS * SLOT, TOK), BF16),
            pltpu.VMEM((2, 3, EXPERTS * SLOT, TOK), BF16),
            pltpu.VMEM((TOK, FEAT), F32),
            dma((6,)),
            dma((NCH,)), dma((NCH,)), dma((NCH,)), dma((NCH,)),
            dma((NCH, 2, 4)), dma((NCH, 2, 4)), dma((NCH, 2, 4)), dma((NCH, 2, 4)),
        ],
        compiler_params=pltpu.CompilerParams(
            collective_id=0, has_side_effects=True, vmem_limit_bytes=60 * 1024 * 1024
        ),
        cost_estimate=pl.CostEstimate(flops=3_200_000_000, bytes_accessed=9_000_000, transcendentals=600_000),
    )(tokens, routes.T, route_weights.T, w_gate, w_up, w_down)


def solution(mesh):
    in_specs = (
        P(("dp", "ctx"), "tensor"),
        P(("dp", "ctx"), None),
        P(("dp", "ctx"), None),
        P("dp", "tensor", None),
        P("dp", "tensor", None),
        P("dp", None, "tensor"),
    )
    return jax.shard_map(
        on_device, mesh=mesh, in_specs=in_specs, out_specs=P(("dp", "ctx"), "tensor"), check_vma=False
    )
```

```python
import functools

import jax
import jax.numpy as jnp
from jax import lax
from jax.experimental import pallas as pl
from jax.experimental.pallas import tpu as pltpu
from jax.sharding import PartitionSpec as P

MESH = pl.DeviceIdType.MESH
BF16, F32 = jnp.bfloat16, jnp.float32

NZ, NX, NXL, NY = 8, 8, 4, 8
EXPERTS, CAP, TOK, TOPK = 32, 12, 160, 2
FEAT, HID = 896, 1536
SLOT, WIDE = 16, 768
TAIL = FEAT - WIDE
COLS = HID // 4

CHUNKS = (
    ((0, 0), (0, 1), (0, 2), (0, 3), (1, 0), (7, 0), (1, 1), (7, 1)),
    ((4, 1), (4, 3), (3, 2), (5, 2), (3, 0), (5, 0), (2, 2), (6, 2)),
    ((4, 2), (4, 0), (3, 3), (5, 3), (3, 1), (5, 1), (2, 3), (6, 3)),
    ((2, 0), (6, 0), (2, 1), (6, 1), (1, 2), (7, 2), (1, 3), (7, 3)),
)
NCH = len(CHUNKS)
ORDER = tuple(offset for chunk in CHUNKS for offset in chunk)
PER = len(ORDER) // NCH
ROWS = PER * CAP
PROWS = PER * SLOT
HALF = ROWS // 2
START = (0, 1, 2, 2)


def dot(a, b):
    return jnp.dot(a, b, preferred_element_type=F32)


def hops(c, d):
    return 4 if (c + d) % 2 == 0 else 3


def kernel(
    tok_hbm, rt_hbm, wt_hbm, wg_hbm, wu_hbm, wd_hbm, out,
    tok, rt, wt, wg, wu, wd, pk, got, part, rs, act, rpk, ret, w_head, w_tail, acc,
    w_sem, d_send, d_recv, r_send, r_recv, s_send, s_recv, g_send, g_recv,
):
    dp, ctx, y = lax.axis_index("dp"), lax.axis_index("ctx"), lax.axis_index("tensor")
    z, xl = lax.div(dp, NXL), lax.rem(dp, NXL)
    xh, core = lax.div(ctx, 2), lax.rem(ctx, 2)
    x = xh * NXL + xl
    turn = 1 - 2 * core
    flip = lax.rem(lax.div(x, 2) + core, 2)
    x_far = lax.rem(x + NX + 2 - 4 * flip, NX)
    x_up, x_down = lax.rem(x + 1, NX), lax.rem(x + NX - 1, NX)

    def device(zz, xx):
        return (
            zz * NXL + lax.rem(xx, NXL),
            lax.div(xx, NXL) * 2 + core,
            y,
        )

    def target(dz, dx):
        return device(lax.rem(z + dz, NZ), (x, x_up, x_far, x_down)[dx])

    def source(dz, dx):
        return device(lax.rem(z + NZ - dz, NZ), (x, x_down, x_far, x_up)[dx])

    y_others = [(dp, ctx, lax.rem(y + k, NY)) for k in (1, NY - 1)]

    inputs = [
        pltpu.make_async_copy(src, dst, w_sem.at[3 + i])
        for i, (src, dst) in enumerate(((rt_hbm, rt), (wt_hbm, wt), (tok_hbm, tok)))
    ]
    loads = [
        pltpu.make_async_copy(src.at[0], dst, w_sem.at[i])
        for i, (src, dst) in enumerate(((wg_hbm, wg), (wu_hbm, wu), (wd_hbm, wd)))
    ]

    for load in inputs + loads:
        load.start()
    barrier = pltpu.get_barrier_semaphore()
    for dz, dx in ORDER:
        if (dz, dx) != (0, 0):
            pl.semaphore_signal(barrier, inc=1, device_id=target(dz, dx), device_id_type=MESH)
    for peer in y_others:
        pl.semaphore_signal(barrier, inc=1, device_id=peer, device_id_type=MESH)

    for load in inputs:
        load.wait()
    block = lax.broadcasted_iota(jnp.int32, (EXPERTS, TOK), 0)
    expert = jnp.zeros((EXPERTS, TOK), jnp.int32)
    for p, (dz, dx) in enumerate(ORDER):
        e = lax.rem(z + dz, NZ) * NXL + lax.rem(xl + dx, NXL)
        expert = jnp.where(block == p, e, expert)
    first, second = rt[0:1, :] == expert, rt[1:2, :] == expert
    named = (first | second).astype(F32)
    earlier = (
        lax.broadcasted_iota(jnp.int32, (TOK, TOK), 0)
        < lax.broadcasted_iota(jnp.int32, (TOK, TOK), 1)
    ).astype(F32).astype(BF16)
    before = dot(named.astype(BF16), earlier)
    slot = jnp.where(first | second, before, -1.0)
    weight = jnp.where(first, wt[0:1, :], jnp.where(second, wt[1:2, :], 0.0))
    q = lax.broadcasted_iota(jnp.int32, (PER, SLOT, TOK), 1).reshape(PROWS, TOK).astype(F32)

    def repeat(values):
        return jnp.broadcast_to(values[:, None, :], (PER, SLOT, TOK)).reshape(PROWS, TOK)

    def masks(c):
        slots = repeat(slot[c * PER : (c + 1) * PER])
        return slots == q, [(slots == q - (CAP - 4 * i)) & (q >= CAP) for i in range(3)]

    def one_hot(mask):
        return mask.astype(F32).astype(BF16)

    def stage_fill(c):
        mine = slice(c * PER, (c + 1) * PER)
        head, tails = masks(c)
        picked = dot(one_hot(head), tok[:, :WIDE])
        for i in range(WIDE // 128):
            piece = picked[:, i * 128 : (i + 1) * 128]
            if i < 3:
                piece = piece + dot(one_hot(tails[i]), tok[:, WIDE:])
            pk[mine, :, i * 128 : (i + 1) * 128] = piece.astype(BF16).reshape(PER, SLOT, 128)

    def stage_dispatch(c):
        for p in range(c * PER, (c + 1) * PER):
            dz, dx = ORDER[p]
            if (dz, dx) == (0, 0):
                pltpu.make_async_copy(pk.at[p], got.at[p], d_recv.at[c]).start()
            else:
                pltpu.make_async_remote_copy(
                    src_ref=pk.at[p], dst_ref=got.at[p], send_sem=d_send.at[c], recv_sem=d_recv.at[c],
                    device_id=target(dz, dx), device_id_type=MESH,
                ).start()

    def stage_weights(c):
        head, tails = masks(c)
        heavy = repeat(weight[c * PER : (c + 1) * PER])
        here = slice(c * PROWS, (c + 1) * PROWS)
        heavy_hi = heavy.astype(BF16).astype(F32)
        for j, part_of in enumerate((heavy_hi, heavy - heavy_hi)):
            w_head[j, here] = jnp.where(head, part_of, 0.0).astype(BF16)
            for i in range(3):
                w_tail[j, i, here] = jnp.where(tails[i], part_of, 0.0).astype(BF16)

    def sent(sem, ref, c):
        remote = sum(ORDER[p] != (0, 0) for p in range(c * PER, (c + 1) * PER))
        span = pl.ds(c * PER, remote)
        pltpu.make_async_copy(ref.at[span], ref.at[span], sem.at[c]).wait()

    stage_fill(0)
    stage_fill(1)
    pl.semaphore_wait(barrier, len(ORDER) - 1 + len(y_others))
    stage_dispatch(0)
    sent(d_send, pk, 0)
    stage_dispatch(1)
    for c in range(2, NCH):
        stage_fill(c)

    def places(shape, packed_axis):
        packed = lax.broadcasted_iota(jnp.int32, shape, packed_axis)
        plain = lax.broadcasted_iota(jnp.int32, shape, 1 - packed_axis)
        start, q = (packed // SLOT) * CAP, packed % SLOT
        kinds = [(plain == start + q) & (q < CAP)]
        kinds += [(plain == start + q - CAP + 4 * i) & (q >= CAP) for i in range(3)]
        return [k.astype(F32).astype(BF16) for k in kinds]

    unpack = places((ROWS, PROWS), 1)
    repack = places((PROWS, ROWS), 0)

    def owned(c, j):
        return act.at[c, j]

    def owner(k, d):
        return lax.rem(y + NY + turn * (k if d == 0 else -k), NY)

    y_to = [(dp, ctx, owner(1, d)) for d in range(2)]

    def sum_copy(c, d, k, src):
        return pltpu.make_async_remote_copy(
            src_ref=src, dst_ref=rs.at[c, d, k - 1], send_sem=s_send.at[c, d, k - 1], recv_sem=s_recv.at[c, d, k - 1],
            device_id=y_to[d], device_id_type=MESH,
        )

    def gather_copy(c, d, k):
        piece = owned(c, owner(k - 1, 1 - d))
        return pltpu.make_async_remote_copy(
            src_ref=piece, dst_ref=piece, send_sem=g_send.at[c, d, k - 1], recv_sem=g_recv.at[c, d, k - 1],
            device_id=y_to[d], device_id_type=MESH,
        )

    def sum_src(c, d, k):
        return part.at[c, owner(hops(c, d), d)] if k == 1 else rs.at[c, d, k - 2]

    def stage_parts(c):
        if c == 1:
            sent(d_send, pk, 1)
            for later in range(2, NCH):
                stage_dispatch(later)
        span = pl.ds(c * PER, PER)
        pltpu.make_async_copy(got.at[span], got.at[span], d_recv.at[c]).wait()
        packed = got[c * PER : (c + 1) * PER].reshape(PROWS, WIDE)
        rows_head = dot(unpack[0], packed).astype(BF16)
        rows_tail = sum(dot(unpack[1 + i], packed[:, i * 128 : (i + 1) * 128]) for i in range(3)).astype(BF16)
        rows = jnp.concatenate([rows_head, rows_tail], axis=1)
        if c == 0:
            loads[0].wait()
            loads[1].wait()

        def columns(it, carry):
            cq = lax.rem(lax.div(y, 2) + 1 + lax.rem(y, 2) + it, 4)
            col = pl.ds(pl.multiple_of(cq * COLS, COLS), COLS)
            for h, w in enumerate((wg, wu)):
                sums = dot(rows, w[:, col]).astype(BF16)
                for rh in range(2):
                    part[c, 2 * cq + rh, h] = sums[rh * HALF : (rh + 1) * HALF]
            return carry

        lax.fori_loop(0, 2, columns, 0)
        for d in range(2):
            sum_copy(c, d, 1, sum_src(c, d, 1)).start()
        lax.fori_loop(2, 4, columns, 0)

    def stage_sum(c, k):
        for d in range(2):
            n = hops(c, d)
            if k > n:
                continue
            sum_copy(c, d, k - 1, sum_src(c, d, k - 1)).wait_recv()
            mine = part[c, owner(n - k + 1, d)].astype(F32)
            rs[c, d, k - 2] = (rs[c, d, k - 2].astype(F32) + mine).astype(BF16)
            sum_copy(c, d, k, sum_src(c, d, k)).start()

    def stage_act(c):
        total = part[c, y].astype(F32)
        for d in range(2):
            n = hops(c, d)
            sum_copy(c, d, n, sum_src(c, d, n)).wait_recv()
            total = total + rs[c, d, n - 1].astype(F32)
        gate, up = total[0], total[1]
        owned(c, y)[...] = (gate / (1.0 + jnp.exp(-gate)) * up).astype(BF16)
        for d in range(2):
            gather_copy(c, d, 1).start()

    def stage_gather(c, k):
        for d in range(2):
            if k > hops(c, d):
                continue
            gather_arrival(c, d, k - 1).wait_recv()
            gather_copy(c, d, k).start()

    def gather_arrival(c, d, k):
        piece = owned(c, owner(k, 1 - d))
        return pltpu.make_async_remote_copy(
            src_ref=piece, dst_ref=piece, send_sem=g_send.at[c, d, k - 1], recv_sem=g_recv.at[c, d, k - 1],
            device_id=y_to[d], device_id_type=MESH,
        )

    def stage_down(c):
        for d in range(2):
            gather_arrival(c, d, hops(c, d)).wait_recv()
        if c == 0:
            loads[2].wait()
        hidden = jnp.concatenate([act[c, j : j + 2].reshape(ROWS, COLS) for j in range(0, NY, 2)], axis=1)
        given = dot(hidden, wd[...]).astype(BF16)
        heads = dot(repack[0], given[:, :WIDE])
        for i in range(WIDE // 128):
            piece = heads[:, i * 128 : (i + 1) * 128]
            if i < 3:
                piece = piece + dot(repack[1 + i], given[:, WIDE:])
            rpk[c * PER : (c + 1) * PER, :, i * 128 : (i + 1) * 128] = piece.astype(BF16).reshape(PER, SLOT, 128)
        for p in range(c * PER, (c + 1) * PER):
            dz, dx = ORDER[p]
            if (dz, dx) == (0, 0):
                pltpu.make_async_copy(rpk.at[p], ret.at[p], r_recv.at[c]).start()
            else:
                pltpu.make_async_remote_copy(
                    src_ref=rpk.at[p], dst_ref=ret.at[p], send_sem=r_send.at[c], recv_sem=r_recv.at[c],
                    device_id=source(dz, dx), device_id_type=MESH,
                ).start()

    def stage_combine(c):
        span = pl.ds(c * PER, PER)
        pltpu.make_async_copy(ret.at[span], ret.at[span], r_recv.at[c]).wait()
        packed = ret[c * PER : (c + 1) * PER].reshape(PROWS, WIDE)
        here = slice(c * PROWS, (c + 1) * PROWS)

        def turned(weights, values):
            return lax.dot_general(weights, values, (((0,), (0,)), ((), ())), preferred_element_type=F32)

        acc[:, :WIDE] += turned(w_head[0, here], packed) + turned(w_head[1, here], packed)
        acc[:, WIDE:] += sum(
            turned(w_tail[j, i, here], packed[:, i * 128 : (i + 1) * 128]) for j in range(2) for i in range(3)
        )

    stages = (
        stage_parts,
        functools.partial(stage_sum, k=2), functools.partial(stage_sum, k=3), functools.partial(stage_sum, k=4),
        stage_act,
        functools.partial(stage_gather, k=2), functools.partial(stage_gather, k=3), functools.partial(stage_gather, k=4),
        stage_down,
    )
    for tick in range(max(START) + len(stages)):
        for c in range(NCH):
            i = tick - START[c]
            if 0 <= i < len(stages):
                stages[i](c)
    for c in range(NCH):
        stage_weights(c)
    acc[...] = jnp.zeros_like(acc)
    for c in range(NCH):
        stage_combine(c)
    out[...] = acc[...].astype(BF16)

    for c in range(NCH):
        if c >= 2:
            sent(d_send, pk, c)
        sent(r_send, rpk, c)
        for d in range(2):
            for k in range(1, hops(c, d) + 1):
                sum_copy(c, d, k, sum_src(c, d, k)).wait_send()
                gather_copy(c, d, k).wait_send()


def on_device(tokens, routes, route_weights, w_gate, w_up, w_down):
    vmem = pl.BlockSpec(memory_space=pltpu.VMEM)
    hbm = pl.BlockSpec(memory_space=pltpu.HBM)
    dma = pltpu.SemaphoreType.DMA
    return pl.pallas_call(
        kernel,
        out_shape=jax.ShapeDtypeStruct((TOK, FEAT), BF16),
        in_specs=[hbm] * 6,
        out_specs=vmem,
        scratch_shapes=[
            pltpu.VMEM((TOK, FEAT), BF16),
            pltpu.VMEM((TOPK, TOK), jnp.int32),
            pltpu.VMEM((TOPK, TOK), F32),
            pltpu.VMEM((FEAT, HID), BF16),
            pltpu.VMEM((FEAT, HID), BF16),
            pltpu.VMEM((HID, FEAT), BF16),
            pltpu.VMEM((EXPERTS, SLOT, WIDE), BF16),
            pltpu.VMEM((EXPERTS, SLOT, WIDE), BF16),
            pltpu.VMEM((NCH, NY, 2, HALF, COLS), BF16),
            pltpu.VMEM((NCH, 2, 4, 2, HALF, COLS), BF16),
            pltpu.VMEM((NCH, NY, HALF, COLS), BF16),
            pltpu.VMEM((EXPERTS, SLOT, WIDE), BF16),
            pltpu.VMEM((EXPERTS, SLOT, WIDE), BF16),
            pltpu.VMEM((2, EXPERTS * SLOT, TOK), BF16),
            pltpu.VMEM((2, 3, EXPERTS * SLOT, TOK), BF16),
            pltpu.VMEM((TOK, FEAT), F32),
            dma((6,)),
            dma((NCH,)), dma((NCH,)), dma((NCH,)), dma((NCH,)),
            dma((NCH, 2, 4)), dma((NCH, 2, 4)), dma((NCH, 2, 4)), dma((NCH, 2, 4)),
        ],
        compiler_params=pltpu.CompilerParams(
            collective_id=0, has_side_effects=True, vmem_limit_bytes=60 * 1024 * 1024
        ),
        cost_estimate=pl.CostEstimate(flops=3_200_000_000, bytes_accessed=9_000_000, transcendentals=600_000),
    )(tokens, routes.T, route_weights.T, w_gate, w_up, w_down)


def solution(mesh):
    in_specs = (
        P(("dp", "ctx"), "tensor"),
        P(("dp", "ctx"), None),
        P(("dp", "ctx"), None),
        P("dp", "tensor", None),
        P("dp", "tensor", None),
        P("dp", None, "tensor"),
    )
    return jax.shard_map(
        on_device, mesh=mesh, in_specs=in_specs, out_specs=P(("dp", "ctx"), "tensor"), check_vma=False
    )
```
